32 devices in a mesh: dp: 2 (over core), ctx: 4 (over y, x), tensor: 4 (over z).
Axes of the slice: x: 2, y: 2, z: 4, core: 2. Of those that a mesh axis runs over, the one named last changes fastest.
Arguments:
- hidden_in: bfloat16 [4, 1024, 2048], P('dp', 'ctx'), may hold values from -6 to 6
- segment_ids: int32 [4, 1024], P('dp', 'ctx'), may hold values from 0 to 21, as said below
- teacher: bfloat16 [4, 1024, 2048], P('dp', 'ctx'), may hold values from -6 to 6
- w_query: bfloat16 [2048, 2048], P(None, 'tensor'), may hold values from -0.125 to 0.125
- b_query: float32 [2048], P('tensor'), may hold values from -1.75 to 1.75
- w_key: bfloat16 [2048, 2048], P(None, 'tensor'), may hold values from -0.125 to 0.125
- w_value: bfloat16 [2048, 2048], P(None, 'tensor'), may hold values from -0.125 to 0.125
- b_value: float32 [2048], P('tensor'), may hold values from -1.75 to 1.75
- w_output: bfloat16 [2048, 2048], P('tensor'), may hold values from -0.75 to 0.75
- b_output: float32 [2048], replicated, may hold values from -1.75 to 1.75
- first_gain: float32 [2048], replicated, may hold values from 0.5 to 1.5
- first_shift: float32 [2048], replicated, may hold values from -1.75 to 1.75
- w_inner: bfloat16 [2048, 8192], P(None, 'tensor'), may hold values from -0.125 to 0.125
- b_inner: float32 [8192], P('tensor'), may hold values from -1.75 to 1.75
- w_outer: bfloat16 [8192, 2048], P('tensor'), may hold values from -0.09375 to 0.09375
- b_outer: float32 [2048], replicated, may hold values from -1.75 to 1.75
- second_gain: float32 [2048], replicated, may hold values from 0.5 to 1.5
- second_shift: float32 [2048], replicated, may hold values from -1.75 to 1.75
Outputs:
- layer_out: bfloat16 [4, 1024, 2048], P('dp', 'ctx')
- loss: float32 [], replicated
- grad_input: float32 [4, 1024, 2048], P('dp', 'ctx')
- grad_w_query: float32 [2048, 2048], P(('dp', 'ctx'), 'tensor')
- grad_b_query: float32 [2048], P('tensor')
- grad_w_key: float32 [2048, 2048], P(('dp', 'ctx'), 'tensor')
- grad_w_value: float32 [2048, 2048], P(('dp', 'ctx'), 'tensor')
- grad_b_value: float32 [2048], P('tensor')
- grad_w_output: float32 [2048, 2048], P('tensor', ('dp', 'ctx'))
- grad_b_output: float32 [2048], replicated
- grad_first_gain: float32 [2048], replicated
- grad_first_shift: float32 [2048], replicated
- grad_w_inner: float32 [2048, 8192], P(('dp', 'ctx'), 'tensor')
- grad_b_inner: float32 [8192], P('tensor')
- grad_w_outer: float32 [8192, 2048], P('tensor', ('dp', 'ctx'))
- grad_b_outer: float32 [2048], replicated
- grad_second_gain: float32 [2048], replicated
- grad_second_shift: float32 [2048], replicated
The draws below stay inside these ranges and needn't reach their ends.
Inputs may be any that keep to these rules, and one draw needn't show every extreme that they name: `segment_ids`: in each sequence the documents are numbered 1, 2, 3 and so on in order, each of 51 to 512 tokens but the last, which may be cut by the padding tail of zeros at the sequence's end (1 to 128 tokens); in each group of 2 consecutive sequences one, drawn, is a single document 1 with no padding.
All inputs are finite; a program needn't handle non-finite values.
Results may differ from the reference program's by a relative error of at most 0.015.
Values may be sent and summed in bfloat16 or wider, within the bound.
A program may use at most 320 MiB of HBM per device.

```python
import jax
import jax.numpy as jnp
from jax import lax

D = 2048
HEADS = 16
HD = 128
FF = 8192
SEQS = 2
SEQUENCES = 4
LENGTH = 1024
TOKENS = 4096
DOC_LO = 51
DOC_HI = 512
N_DP = 2


def draw_segment_ids(key, part):
    key = jax.random.fold_in(key, 11)
    row_count = SEQS * N_DP
    doc_slots = LENGTH // DOC_LO + 2
    key_sizes, key_tail, key_pick = jax.random.split(key, 3)
    doc_sizes = jax.random.randint(key_sizes, (row_count, doc_slots), DOC_LO, DOC_HI + 1)
    doc_ends = jnp.cumsum(doc_sizes, axis=1)
    places = jnp.arange(LENGTH)
    number = 1 + jnp.sum((doc_ends[:, None, :] <= places[None, :, None]).astype(jnp.int32), axis=2)
    tail_len = jax.random.randint(key_tail, (row_count, 1), 1, LENGTH // 8 + 1)
    number = jnp.where(places[None, :] >= LENGTH - tail_len, 0, number)
    chosen = jax.random.randint(key_pick, (N_DP, 1), 0, SEQS)
    if SEQS > 1:
        densest = jnp.where(places == LENGTH - 1, 0, 1 + places // DOC_LO)
        dense_pick = (jnp.arange(SEQS)[None, :] == (chosen + 1) % SEQS).reshape(row_count, 1)
        number = jnp.where(dense_pick, densest[None, :], number)
    single_doc = (jnp.arange(SEQS)[None, :] == chosen).reshape(row_count, 1)
    return jnp.where(single_doc, 1, number).astype(jnp.int32)


def steps_of(own_key, extent, cuts, low, largest):
    def one(axis_at, parts):
        heights = jax.random.uniform(jax.random.fold_in(jax.random.fold_in(own_key, 6), axis_at), (parts,), jnp.float32, low / len(cuts), largest / len(cuts))
        return jnp.repeat(jnp.exp(heights), extent[axis_at] // parts).reshape((-1,) + (1,) * (len(extent) - axis_at - 1))

    loudness = one(*cuts[0])
    for cut in cuts[1:]:
        loudness = loudness * one(*cut)
    return loudness


def noise(key, shape, width, bound, shards=(), dtype=jnp.bfloat16):
    values = width * jax.random.normal(key, shape, jnp.float32)
    if shards:
        values = values * steps_of(key, shape, shards, -0.22, 0.18)
    return jnp.clip(values, -bound, bound).astype(dtype)


def setup_inputs(seed: int = 0) -> dict:
    splits = jax.random.split(jax.random.key(seed), 19)
    return {
        "hidden_in": noise(splits[0], (SEQUENCES, LENGTH, D), 1.0, 6.0, ((0, 2), (1, 4))),
        "segment_ids": draw_segment_ids(jax.random.fold_in(splits[18], 71), 0),
        "teacher": noise(splits[2], (SEQUENCES, LENGTH, D), 1.0, 6.0, ((0, 2), (1, 4))),
        "w_query": noise(splits[3], (D, D), D ** -0.5, 0.125, ((1, 4),)),
        "b_query": noise(splits[4], (D,), 0.3, 1.75, ((0, 4),), jnp.float32),
        "w_key": noise(splits[5], (D, D), D ** -0.5, 0.125, ((1, 4),)),
        "w_value": noise(splits[6], (D, D), D ** -0.5, 0.125, ((1, 4),)),
        "b_value": noise(splits[7], (D,), 0.3, 1.75, ((0, 4),), jnp.float32),
        "w_output": noise(splits[8], (D, D), (D // 32) ** -0.5, 0.75, ((0, 4),)),
        "b_output": noise(splits[9], (D,), 0.3, 1.75, (), jnp.float32),
        "first_gain": jnp.clip(1.0 + 0.1 * jax.random.normal(splits[10], (D,), jnp.float32), 0.5, 1.5),
        "first_shift": noise(splits[11], (D,), 0.3, 1.75, (), jnp.float32),
        "w_inner": noise(splits[12], (D, FF), D ** -0.5, 0.125, ((1, 4),)),
        "b_inner": noise(splits[13], (FF,), 0.3, 1.75, ((0, 4),), jnp.float32),
        "w_outer": noise(splits[14], (FF, D), (FF // 2) ** -0.5, 0.09375, ((0, 4),)),
        "b_outer": noise(splits[15], (D,), 0.3, 1.75, (), jnp.float32),
        "second_gain": jnp.clip(1.0 + 0.1 * jax.random.normal(splits[16], (D,), jnp.float32), 0.5, 1.5),
        "second_shift": noise(splits[17], (D,), 0.3, 1.75, (), jnp.float32),
    }


@jax.custom_vjp
def low(v):
    return lax.optimization_barrier(v.astype(jnp.bfloat16)).astype(jnp.float32)

@jax.custom_vjp
def low_back(v):
    return v

def low_keep(v):
    return (low(v), None)

def low_pass(kept, grad):
    return (grad,)

def back_keep(v):
    return (v, None)

def back_low(kept, grad):
    return (low(grad),)
low.defvjp(low_keep, low_pass)
low_back.defvjp(back_keep, back_low)

def matmul(left, right):
    return jnp.dot(left, right, precision=lax.Precision.HIGHEST, preferred_element_type=jnp.float32)

def layer_norm(values, gain, shift):
    center = values - lax.optimization_barrier(jnp.mean(values, axis=-1, keepdims=True))
    spread = lax.optimization_barrier(jnp.mean(center * center, axis=-1, keepdims=True))
    return center * lax.rsqrt(spread + 1e-05) * gain + shift

def activate(values):
    return jax.nn.gelu(values, approximate=True)

def one_sequence(params, seq_in, seq_ids, seq_target):
    w_query, b_query, w_key, w_value, b_value, w_output, b_output, first_gain, first_shift, w_inner, b_inner, w_outer, b_outer, second_gain, second_shift = params
    queries = low_back(low(matmul(seq_in, w_query) + b_query))
    key_rows = low_back(low(matmul(seq_in, w_key)))
    value_rows = low_back(low(matmul(seq_in, w_value) + b_value))
    key_heads = key_rows.reshape(LENGTH, HEADS, HD)
    value_heads = value_rows.reshape(LENGTH, HEADS, HD)
    score_scale = HD ** (-0.5)
    block_len = 512 if LENGTH % 512 == 0 else LENGTH

    def attend_block(block_item):
        block_query, block_ids = block_item
        score = jnp.einsum('qhd,khd->hqk', block_query, key_heads, precision=lax.Precision.HIGHEST) * score_scale
        score = low_back(score)
        same_doc = block_ids[None, :, None] == seq_ids[None, None, :]
        score = jnp.where(same_doc, score, -1e+30)
        row_max = lax.optimization_barrier(jnp.max(score, axis=-1, keepdims=True))
        log_total = row_max + jnp.log(lax.optimization_barrier(jnp.sum(jnp.exp(score - row_max), axis=-1, keepdims=True)))
        weights = low(jnp.exp(score - log_total))
        return jnp.einsum('hqk,khd->qhd', weights, value_heads, precision=lax.Precision.HIGHEST)
    block_count = LENGTH // block_len
    attended = lax.map(jax.checkpoint(attend_block), (queries.reshape(block_count, block_len, HEADS, HD), seq_ids.reshape(block_count, block_len)))
    attended = low_back(low(attended.reshape(LENGTH, D)))
    mixed_sum = low_back(matmul(attended, w_output) + b_output)
    normed = layer_norm(seq_in + mixed_sum, first_gain, first_shift)
    pre_act = low_back(matmul(low(normed), w_inner) + b_inner)
    hidden_act = low(activate(pre_act))
    outer_sum = low_back(matmul(hidden_act, w_outer) + b_outer)
    result = layer_norm(normed + outer_sum, second_gain, second_shift)
    valid_rows = (seq_ids > 0).astype(jnp.float32)
    error_gap = result - seq_target
    error_sum = jnp.sum(valid_rows[:, None] * error_gap * error_gap)
    return (result, error_sum)

def reference(hidden_in, segment_ids, teacher, w_query, b_query, w_key, w_value, b_value, w_output, b_output, first_gain, first_shift, w_inner, b_inner, w_outer, b_outer, second_gain, second_shift):
    params = tuple((weight.astype(jnp.float32) for weight in (w_query, b_query, w_key, w_value, b_value, w_output, b_output, first_gain, first_shift, w_inner, b_inner, w_outer, b_outer, second_gain, second_shift)))
    inputs = hidden_in.astype(jnp.float32)
    targets = teacher.astype(jnp.float32)
    total_count = jnp.sum((segment_ids > 0).astype(jnp.float32))

    def total_loss(layer_in, weights):

        def seq_step(running, seq_item):
            seq_out, seq_error = jax.checkpoint(one_sequence)(weights, seq_item[0], seq_item[1], seq_item[2])
            return (running + seq_error, seq_out)
        error_sum, outputs = lax.scan(seq_step, jnp.zeros((), jnp.float32), (layer_in, segment_ids, targets))
        return (TOKENS * error_sum / total_count, (outputs, error_sum))
    scaled, pull_back, extras = jax.vjp(total_loss, inputs, params, has_aux=True)
    grad_input, grads = pull_back(jnp.ones((), jnp.float32))
    outputs, error_sum = extras
    return (outputs.astype(jnp.bfloat16), error_sum / total_count, grad_input, grads[0], grads[1], grads[2], grads[3], grads[4], grads[5], grads[6], grads[7], grads[8], grads[9], grads[10], grads[11], grads[12], grads[13], grads[14])
```

```python
import jax
import jax.numpy as jnp
from jax import lax
from jax.experimental import pallas as pl
from jax.experimental.pallas import tpu as pltpu
from jax.sharding import PartitionSpec as P

HD = 128
VMEM_BYTES = 63 * 2**20
GELU_A = 0.7978845608028654


def layer_norm(values, gain, shift):
    center = values - jnp.mean(values, axis=-1, keepdims=True)
    spread = jnp.mean(center * center, axis=-1, keepdims=True)
    return center * lax.rsqrt(spread + 1e-05) * gain + shift


def activate(values):
    return jax.nn.gelu(values, approximate=True)


def outer_sum(left, right):
    return jnp.einsum("rd,re->de", left, right, preferred_element_type=jnp.float32)


def column_sum(values):
    return jnp.sum(values.astype(jnp.float32), axis=0)


def masked_scores(queries, key_heads, query_ids, key_ids):
    score_scale = queries.shape[-1] ** (-0.5)
    score = (
        jnp.einsum("qhd,khd->hqk", queries, key_heads, preferred_element_type=jnp.float32)
        * score_scale
    )
    same_doc = query_ids[None, :, None] == key_ids[None, None, :]
    return jnp.where(same_doc, score, -1e30)


def forward_one(seq_item):
    queries, key_heads, value_heads, query_ids, key_ids = seq_item
    score = masked_scores(queries, key_heads, query_ids, key_ids)
    row_max = jnp.max(score, axis=-1, keepdims=True)
    log_total = row_max + jnp.log(jnp.sum(jnp.exp(score - row_max), axis=-1, keepdims=True))
    weights = jnp.exp(score - log_total).astype(jnp.bfloat16)
    attended = jnp.einsum("hqk,khd->qhd", weights, value_heads, preferred_element_type=jnp.float32)
    return (attended.astype(jnp.bfloat16), log_total)


def backward_one(seq_item):
    queries, key_heads, value_heads, query_ids, key_ids, log_total, d_attended = seq_item
    score_scale = queries.shape[-1] ** (-0.5)
    score = masked_scores(queries, key_heads, query_ids, key_ids)
    probs = jnp.exp(score - log_total)
    d_probs = jnp.einsum(
        "qhd,khd->hqk", d_attended, value_heads, preferred_element_type=jnp.float32
    )
    inner = jnp.sum(probs * d_probs, axis=-1, keepdims=True)
    d_score = (probs * (d_probs - inner)).astype(jnp.bfloat16)
    d_query = (
        jnp.einsum("hqk,khd->qhd", d_score, key_heads, preferred_element_type=jnp.float32)
        * score_scale
    )
    d_key = (
        jnp.einsum("hqk,qhd->khd", d_score, queries, preferred_element_type=jnp.float32)
        * score_scale
    )
    d_value = jnp.einsum(
        "hqk,qhd->khd", probs.astype(jnp.bfloat16), d_attended, preferred_element_type=jnp.float32
    )
    return (d_query, d_key, d_value)


def shards(
    hidden_in,
    segment_ids,
    teacher,
    w_query,
    b_query,
    w_key,
    w_value,
    b_value,
    w_output,
    b_output,
    first_gain,
    first_shift,
    w_inner,
    b_inner,
    w_outer,
    b_outer,
    second_gain,
    second_shift,
):
    seq_count, span_len, model_width = hidden_in.shape
    row_count = seq_count * span_len
    local_width = w_query.shape[1]
    head_count = local_width // HD
    inputs = hidden_in.reshape(row_count, model_width)
    queries = (jnp.dot(inputs, w_query, preferred_element_type=jnp.float32) + b_query).astype(
        jnp.bfloat16
    )
    key_rows = jnp.dot(inputs, w_key, preferred_element_type=jnp.float32).astype(jnp.bfloat16)
    value_rows = (jnp.dot(inputs, w_value, preferred_element_type=jnp.float32) + b_value).astype(
        jnp.bfloat16
    )
    key_local = key_rows.reshape(seq_count, span_len, local_width)
    value_local = value_rows.reshape(seq_count, span_len, local_width)

    def heads_view(block_in):
        return block_in.reshape(block_in.shape[0], block_in.shape[1], head_count, HD)

    gathered = (
        lax.all_gather(key_local, "ctx", axis=1, tiled=True),
        lax.all_gather(value_local, "ctx", axis=1, tiled=True),
        lax.all_gather(segment_ids, "ctx", axis=1, tiled=True),
    )
    query_heads = heads_view(queries.reshape(seq_count, span_len, local_width))
    attended, log_total = lax.map(
        forward_one,
        (query_heads, heads_view(gathered[0]), heads_view(gathered[1]), segment_ids, gathered[2]),
    )
    attn_rows = attended.reshape(row_count, local_width)
    mixed_sum = (
        lax.psum(jnp.dot(attn_rows, w_output, preferred_element_type=jnp.float32), "tensor")
        + b_output
    )
    first_sum = inputs.astype(jnp.float32) + mixed_sum
    normed, first_back = jax.vjp(layer_norm, first_sum, first_gain, first_shift)
    normed_low = normed.astype(jnp.bfloat16)
    pre_act = jnp.dot(normed_low, w_inner, preferred_element_type=jnp.float32) + b_inner
    hidden_act, gelu_back = jax.vjp(activate, pre_act)
    act_low = hidden_act.astype(jnp.bfloat16)
    outer_part = (
        lax.psum(jnp.dot(act_low, w_outer, preferred_element_type=jnp.float32), "tensor") + b_outer
    )
    result, second_back = jax.vjp(layer_norm, normed + outer_part, second_gain, second_shift)
    valid_rows = (segment_ids.reshape(row_count) > 0).astype(jnp.float32)
    error_gap = result - teacher.reshape(row_count, model_width).astype(jnp.float32)
    error_sum, total_count = lax.psum(
        (jnp.sum(valid_rows[:, None] * error_gap * error_gap), jnp.sum(valid_rows)), ("dp", "ctx")
    )
    loss = error_sum / total_count
    token_slots = row_count * lax.axis_size("dp") * lax.axis_size("ctx")
    d_result = 2.0 * token_slots / total_count * valid_rows[:, None] * error_gap
    d_second, grad_second_gain, grad_second_shift = second_back(d_result)
    d_outer_low = d_second.astype(jnp.bfloat16)
    grad_b_outer = column_sum(d_outer_low)
    grad_w_outer = outer_sum(act_low, d_outer_low)
    d_act = jnp.dot(d_outer_low, w_outer.T, preferred_element_type=jnp.float32)
    d_pre_low = gelu_back(d_act)[0].astype(jnp.bfloat16)
    grad_b_inner = column_sum(d_pre_low)
    grad_w_inner = outer_sum(normed_low, d_pre_low)
    d_normed = d_second + lax.psum(
        jnp.dot(d_pre_low, w_inner.T, preferred_element_type=jnp.float32), "tensor"
    )
    d_first, grad_first_gain, grad_first_shift = first_back(d_normed)
    d_mixed_low = d_first.astype(jnp.bfloat16)
    grad_b_output = column_sum(d_mixed_low)
    grad_w_output = outer_sum(attn_rows, d_mixed_low)
    d_attended = jnp.dot(d_mixed_low, w_output.T, preferred_element_type=jnp.float32).astype(
        jnp.bfloat16
    )
    d_attended_heads = heads_view(d_attended.reshape(seq_count, span_len, local_width))
    gathered = (
        lax.all_gather(key_local, "ctx", axis=1, tiled=True),
        lax.all_gather(value_local, "ctx", axis=1, tiled=True),
        lax.all_gather(segment_ids, "ctx", axis=1, tiled=True),
    )
    d_query, d_key_all, d_value_all = lax.map(
        backward_one,
        (
            query_heads,
            heads_view(gathered[0]),
            heads_view(gathered[1]),
            segment_ids,
            gathered[2],
            log_total,
            d_attended_heads,
        ),
    )
    d_key_part, d_value_part = (
        lax.psum_scatter(d_key_all, "ctx", scatter_dimension=1, tiled=True),
        lax.psum_scatter(d_value_all, "ctx", scatter_dimension=1, tiled=True),
    )
    d_query_low = d_query.reshape(row_count, local_width).astype(jnp.bfloat16)
    d_key_low = d_key_part.reshape(row_count, local_width).astype(jnp.bfloat16)
    d_value_low = d_value_part.reshape(row_count, local_width).astype(jnp.bfloat16)
    grad_b_query = column_sum(d_query_low)
    grad_b_value = column_sum(d_value_low)
    grad_w_query = outer_sum(inputs, d_query_low)
    grad_w_key = outer_sum(inputs, d_key_low)
    grad_w_value = outer_sum(inputs, d_value_low)
    back_in = jnp.dot(d_query_low, w_query.T, preferred_element_type=jnp.float32)
    back_in = back_in + jnp.dot(d_key_low, w_key.T, preferred_element_type=jnp.float32)
    back_in = back_in + jnp.dot(d_value_low, w_value.T, preferred_element_type=jnp.float32)
    grad_input = d_first + lax.psum(back_in, "tensor")
    grad_w_query, grad_w_key, grad_w_value, grad_w_output, grad_w_inner, grad_w_outer = (
        lax.psum_scatter(grad_w_query, ("dp", "ctx"), scatter_dimension=0, tiled=True),
        lax.psum_scatter(grad_w_key, ("dp", "ctx"), scatter_dimension=0, tiled=True),
        lax.psum_scatter(grad_w_value, ("dp", "ctx"), scatter_dimension=0, tiled=True),
        lax.psum_scatter(grad_w_output, ("dp", "ctx"), scatter_dimension=1, tiled=True),
        lax.psum_scatter(grad_w_inner, ("dp", "ctx"), scatter_dimension=0, tiled=True),
        lax.psum_scatter(grad_w_outer, ("dp", "ctx"), scatter_dimension=1, tiled=True),
    )
    (
        grad_b_query,
        grad_b_value,
        grad_b_output,
        grad_first_gain,
        grad_first_shift,
        grad_b_inner,
        grad_b_outer,
        grad_second_gain,
        grad_second_shift,
    ) = (
        lax.psum(grad_b_query.astype(jnp.bfloat16), ("dp", "ctx")).astype(jnp.float32),
        lax.psum(grad_b_value.astype(jnp.bfloat16), ("dp", "ctx")).astype(jnp.float32),
        lax.psum(grad_b_output.astype(jnp.bfloat16), ("dp", "ctx")).astype(jnp.float32),
        lax.psum(grad_first_gain.astype(jnp.bfloat16), ("dp", "ctx")).astype(jnp.float32),
        lax.psum(grad_first_shift.astype(jnp.bfloat16), ("dp", "ctx")).astype(jnp.float32),
        lax.psum(grad_b_inner.astype(jnp.bfloat16), ("dp", "ctx")).astype(jnp.float32),
        lax.psum(grad_b_outer.astype(jnp.bfloat16), ("dp", "ctx")).astype(jnp.float32),
        lax.psum(grad_second_gain.astype(jnp.bfloat16), ("dp", "ctx")).astype(jnp.float32),
        lax.psum(grad_second_shift.astype(jnp.bfloat16), ("dp", "ctx")).astype(jnp.float32),
    )
    layer_out = result.astype(jnp.bfloat16).reshape(seq_count, span_len, model_width)
    return (
        layer_out,
        loss,
        grad_input.reshape(seq_count, span_len, model_width),
        grad_w_query,
        grad_b_query,
        grad_w_key,
        grad_w_value,
        grad_b_value,
        grad_w_output,
        grad_b_output,
        grad_first_gain,
        grad_first_shift,
        grad_w_inner,
        grad_b_inner,
        grad_w_outer,
        grad_b_outer,
        grad_second_gain,
        grad_second_shift,
    )


MESH = pl.DeviceIdType.MESH
F32 = jnp.float32
BF16 = jnp.bfloat16
CHUNKS = 8


def place():
    return lax.axis_index("dp"), lax.axis_index("ctx"), lax.axis_index("tensor")


def dot(left, right):
    return lax.dot_general(left, right, (((1,), (0,)), ((), ())), preferred_element_type=F32)


def dot_nt(left, right):
    return lax.dot_general(left, right, (((1,), (1,)), ((), ())), preferred_element_type=F32)


def dot_tn(left, right):
    return lax.dot_general(left, right, (((0,), (0,)), ((), ())), preferred_element_type=F32)


def remote(src, dst, send, recv, device):
    return pltpu.make_async_remote_copy(
        src_ref=src,
        dst_ref=dst,
        send_sem=send,
        recv_sem=recv,
        device_id=device,
        device_id_type=MESH,
    )


def greet(always, line):
    d, c, t = place()
    barrier = pltpu.get_barrier_semaphore()
    for device in always:
        pl.semaphore_signal(barrier, inc=1, device_id=device, device_id_type=MESH)
    if line:
        last = lax.axis_size("tensor") - 1

        @pl.when(t < last)
        def _():
            pl.semaphore_signal(
                barrier, inc=1, device_id=(d, c, jnp.minimum(t + 1, last)), device_id_type=MESH
            )

        @pl.when(t > 0)
        def _():
            pl.semaphore_signal(
                barrier, inc=1, device_id=(d, c, jnp.maximum(t - 1, 0)), device_id_type=MESH
            )

    expected = len(always)
    if line:
        expected = expected + (t < last).astype(jnp.int32) + (t > 0).astype(jnp.int32)
    pl.semaphore_wait(barrier, expected)


def ctx_peers():
    d, c, t = place()
    return [(d, 3 - c, t), (d, c + 1 - 2 * lax.rem(c, 2), t), (d, lax.rem(c + 2, 4), t)]


def line_sum(produce, line, beside=()):
    sent, got, middle_got, total = line[:4]
    end_send, end_recv, red_send, red_recv, out_send, out_recv, back_send, back_recv = line[4:]
    d, c, t = place()
    is_end = (t == 0) | (t == 3)
    near = (t >= 2).astype(jnp.int32)
    far = 1 - near
    partner = (d, c, t + 1 - 2 * lax.rem(t, 2))
    across = (d, c, 3 - t)

    def end_copy(half, chunk):
        return remote(
            sent.at[half, chunk],
            got.at[half, chunk],
            end_send.at[half, chunk],
            end_recv.at[half, chunk],
            partner,
        )

    def reduce_copy(chunk):
        return remote(
            sent.at[far, chunk], middle_got.at[chunk], red_send.at[chunk], red_recv.at[chunk], across
        )

    def out_copy(half, chunk):
        return remote(
            total.at[half, chunk],
            total.at[half, chunk],
            out_send.at[half, chunk],
            out_recv.at[half, chunk],
            across,
        )

    def back_copy(half, chunk):
        return remote(
            total.at[half, chunk],
            total.at[half, chunk],
            back_send.at[half, chunk],
            back_recv.at[half, chunk],
            partner,
        )

    def inside(chunk):
        return (chunk >= 0) & (chunk < CHUNKS)

    def step(s, carry):
        @pl.when(is_end & inside(s))
        def _():
            for half in (far, near):
                sent[half, s] = produce(half, s).astype(BF16)
                end_copy(half, s).start()

        @pl.when(jnp.logical_not(is_end))
        def _():
            @pl.when(inside(s - 1))
            def _():
                chunk = s - 1
                value = produce(far, chunk)
                end_copy(far, chunk).wait_recv()
                sent[far, chunk] = (value + got[far, chunk].astype(F32)).astype(BF16)
                reduce_copy(chunk).start()

            @pl.when(inside(s - 2))
            def _():
                chunk = s - 2
                value = produce(near, chunk)
                end_copy(near, chunk).wait_recv()
                value = value + got[near, chunk].astype(F32)
                reduce_copy(chunk).wait_recv()
                total[near, chunk] = (value + middle_got[chunk].astype(F32)).astype(BF16)
                out_copy(near, chunk).start()
                back_copy(near, chunk).start()

            @pl.when(inside(s - 3))
            def _():
                out_copy(far, s - 3).wait_recv()
                back_copy(far, s - 3).start()

        for at, task in beside:
            pl.when(s == at)(task)
        return carry

    lax.fori_loop(0, CHUNKS + 3, step, 0)

    def drain(chunk, carry):
        @pl.when(is_end)
        def _():
            for half in (near, far):
                back_copy(half, chunk).wait_recv()
                end_copy(half, chunk).wait_send()

        @pl.when(jnp.logical_not(is_end))
        def _():
            reduce_copy(chunk).wait_send()
            out_copy(near, chunk).wait_send()
            for half in (near, far):
                back_copy(half, chunk).wait_send()

        return carry

    lax.fori_loop(0, CHUNKS, drain, 0)


def line_scratch(rows, width):
    half = rows // 2
    columns = width // CHUNKS
    block = pltpu.VMEM((2, CHUNKS, half, columns), BF16)
    pair, single = pltpu.SemaphoreType.DMA((2, CHUNKS)), pltpu.SemaphoreType.DMA((CHUNKS,))
    return [block, block, pltpu.VMEM((CHUNKS, half, columns), BF16), block] + [
        pair, pair, single, single, pair, pair, pair, pair
    ]


LINE_REFS = 12


STEP_ROWS = 32


def row_block(total, step):
    per_half = total.shape[2] // STEP_ROWS
    half = step // per_half
    start = pl.multiple_of((step - half * per_half) * STEP_ROWS, STEP_ROWS)
    return jnp.concatenate(
        [total[half, chunk, pl.ds(start, STEP_ROWS), :] for chunk in range(CHUNKS)], axis=1
    ).astype(F32)


def rows_at(step):
    return pl.ds(pl.multiple_of(step * STEP_ROWS, STEP_ROWS), STEP_ROWS)


def fold(values):
    return jnp.sum(values.reshape(values.shape[0] // 8, 8, values.shape[1]), axis=0)


def mean_last(values):
    return jnp.mean(values, axis=-1, keepdims=True)


def scatter_scratch(tiles, rows, columns):
    return [
        pltpu.VMEM((2, tiles, rows, columns), BF16),
        pltpu.VMEM((4, tiles, rows, columns), BF16),
        pltpu.VMEM((3, tiles, rows, columns), BF16),
        pltpu.VMEM((3, tiles, rows, columns), BF16),
        pltpu.SemaphoreType.DMA((4,)),
        pltpu.SemaphoreType.DMA((4,)),
        pltpu.SemaphoreType.DMA((3,)),
        pltpu.SemaphoreType.DMA((3,)),
    ]


SCATTER_REFS = 8


class Scatter:
    def __init__(self, compute, read, write, refs):
        self.compute, self.read, self.write = compute, read, write
        self.core_out, self.core_in, self.cross_out, self.cross_in = refs[:4]
        self.core_send, self.core_recv, self.cross_send, self.cross_recv = refs[4:]
        self.tiles = self.core_in.shape[1]
        d, c, t = place()
        self.core = d
        self.other = (1 - d, c, t)
        self.peers = ctx_peers()
        self.targets = [peer[1] for peer in self.peers] + [c]

    def core_copy(self, unit):
        return remote(
            self.core_out.at[unit % 2],
            self.core_in.at[unit],
            self.core_send.at[unit],
            self.core_recv.at[unit],
            self.other,
        )

    def cross_copy(self, unit):
        return remote(
            self.cross_out.at[unit],
            self.cross_in.at[unit],
            self.cross_send.at[unit],
            self.cross_recv.at[unit],
            self.peers[unit],
        )

    def loop(self, body):
        def step(tile, carry):
            body(tile)
            return carry

        lax.fori_loop(0, self.tiles, step, 0)

    def give(self, unit):
        if unit >= 2:
            self.core_copy(unit - 2).wait_send()

        def body(tile):
            value = self.compute(1 - self.core, self.targets[unit], tile)
            self.core_out[unit % 2, tile] = value.astype(BF16)

        self.loop(body)
        self.core_copy(unit).start()

    def take(self, unit):
        self.core_copy(unit).wait_recv()

        def body(tile):
            value = self.compute(self.core, self.targets[unit], tile)
            value = value + self.core_in[unit, tile].astype(F32)
            if unit < 3:
                self.cross_out[unit, tile] = value.astype(BF16)
            else:
                self.write(tile, value)

        self.loop(body)
        if unit < 3:
            self.cross_copy(unit).start()

    def finish(self):
        for unit in range(3):
            self.cross_copy(unit).wait_recv()

        def body(tile):
            value = self.read(tile)
            for unit in range(3):
                value = value + self.cross_in[unit, tile].astype(F32)
            self.write(tile, value)

        self.loop(body)
        for unit in range(3):
            self.cross_copy(unit).wait_send()
        self.core_copy(2).wait_send()
        self.core_copy(3).wait_send()

    def pairs(self):
        def both(unit):
            def run():
                if unit < 3:
                    self.give(unit + 1)
                self.take(unit)

            return run

        return [both(unit) for unit in range(4)]


def tile_at(index, size):
    return pl.ds(pl.multiple_of(index * size, size), size)


def id_columns(row):
    return jnp.broadcast_to(row, (128, row.shape[1])).T[:, :1]


PIECES = 8


class Line:
    def __init__(self, refs, produce):
        self.sent, self.got, self.middle_got, self.total = refs[:4]
        (
            self.end_send,
            self.end_recv,
            self.red_send,
            self.red_recv,
            self.out_send,
            self.out_recv,
            self.back_send,
            self.back_recv,
        ) = refs[4:]
        self.produce = produce
        d, c, t = place()
        self.is_end = (t == 0) | (t == 3)
        self.near = (t >= 2).astype(jnp.int32)
        self.far = 1 - self.near
        self.partner = (d, c, t + 1 - 2 * lax.rem(t, 2))
        self.across = (d, c, 3 - t)

    def end_copy(self, half, piece):
        return remote(
            self.sent.at[half, piece],
            self.got.at[half, piece],
            self.end_send.at[half, piece],
            self.end_recv.at[half, piece],
            self.partner,
        )

    def reduce_copy(self, piece):
        return remote(
            self.sent.at[self.far, piece],
            self.middle_got.at[piece],
            self.red_send.at[piece],
            self.red_recv.at[piece],
            self.across,
        )

    def out_copy(self, half, piece):
        return remote(
            self.total.at[half, piece],
            self.total.at[half, piece],
            self.out_send.at[half, piece],
            self.out_recv.at[half, piece],
            self.across,
        )

    def back_copy(self, half, piece):
        return remote(
            self.total.at[half, piece],
            self.total.at[half, piece],
            self.back_send.at[half, piece],
            self.back_recv.at[half, piece],
            self.partner,
        )

    def step(self, s):
        near, far = self.near, self.far

        def inside(piece):
            return (piece >= 0) & (piece < PIECES)

        @pl.when(self.is_end & inside(s))
        def _():
            for half in (far, near):
                self.sent[half, s] = self.produce(half, s).astype(BF16)
                self.end_copy(half, s).start()

        @pl.when(jnp.logical_not(self.is_end))
        def _():
            @pl.when(inside(s - 1))
            def _():
                piece = s - 1
                value = self.produce(far, piece)
                self.end_copy(far, piece).wait_recv()
                self.sent[far, piece] = (value + self.got[far, piece].astype(F32)).astype(BF16)
                self.reduce_copy(piece).start()

            @pl.when(inside(s - 2))
            def _():
                piece = s - 2
                value = self.produce(near, piece)
                self.end_copy(near, piece).wait_recv()
                value = value + self.got[near, piece].astype(F32)
                self.reduce_copy(piece).wait_recv()
                value = value + self.middle_got[piece].astype(F32)
                self.total[near, piece] = value.astype(BF16)
                self.out_copy(near, piece).start()
                self.back_copy(near, piece).start()

            @pl.when(inside(s - 3))
            def _():
                self.out_copy(far, s - 3).wait_recv()
                self.back_copy(far, s - 3).start()

    def arrived(self):
        @pl.when(self.is_end)
        def _():
            def body(piece, carry):
                self.back_copy(self.near, piece).wait_recv()
                self.back_copy(self.far, piece).wait_recv()
                return carry

            lax.fori_loop(0, PIECES, body, 0)

    def drain(self):
        def body(piece, carry):
            @pl.when(self.is_end)
            def _():
                self.end_copy(self.near, piece).wait_send()
                self.end_copy(self.far, piece).wait_send()

            @pl.when(jnp.logical_not(self.is_end))
            def _():
                self.reduce_copy(piece).wait_send()
                self.out_copy(self.near, piece).wait_send()
                self.back_copy(self.near, piece).wait_send()
                self.back_copy(self.far, piece).wait_send()

            return carry

        lax.fori_loop(0, PIECES, body, 0)

    def rows(self, start):
        return jnp.concatenate(
            [
                self.total[half, piece, pl.ds(start, STEP_ROWS), :]
                for half in range(2)
                for piece in range(PIECES)
            ],
            axis=1,
        ).astype(F32)


def stream_scratch(span, width):
    columns = width // (2 * PIECES)
    block = pltpu.VMEM((2, PIECES, span, columns), BF16)
    pair, single = pltpu.SemaphoreType.DMA((2, PIECES)), pltpu.SemaphoreType.DMA((PIECES,))
    return [block, block, pltpu.VMEM((PIECES, span, columns), BF16), block] + [
        pair, pair, single, single, pair, pair, pair, pair
    ]


def run_stream(lines, tasks):
    for k, line in enumerate(lines):

        def step(j, carry, k=k, line=line):
            if k > 0:
                lines[k - 1].step(j + PIECES)
            line.step(j)
            for at, task in tasks[k]:
                pl.when(j == at)(task)
            return carry

        lax.fori_loop(0, PIECES, step, 0)

    def last(j, carry):
        lines[-1].step(j + PIECES)
        return carry

    lax.fori_loop(0, 3, last, 0)


def each_block(span, body):
    def step(i, carry):
        body(pl.multiple_of(i * STEP_ROWS, STEP_ROWS))
        return carry

    lax.fori_loop(0, span // STEP_ROWS, step, 0)


def forward_kernel(
    x_hbm, ids_ref, valid_ref, wq_hbm, wk_hbm, wv_hbm, bias_ref, wo_hbm, wi_hbm, bi_ref, wf_hbm, teacher_hbm, vec_ref,
    all_ids_ref, qkv_hbm, lse_ref, o_hbm, low_hbm, out_hbm, dpre_hbm, dmix_hbm, sums_ref, bsum_ref, error_ref, gouter_hbm,
    x_ref, wf_ref, wi_ref, wo_ref, qkv_ref, psend, o_ref, osend, norm_ref, rstd_ref, low_ref, act_ref, slope_ref, dlow_ref, mix_ref, gouter_ref,
    lsem, wsem, pssem, prsem, isem, jsem, ossem, orsem, *refs,
):
    d, c, t = place()
    span = ids_ref.shape[1]
    local = wi_ref.shape[1]
    width = x_ref.shape[1]
    peers = ctx_peers()
    targets = [peer[1] for peer in peers] + [c]
    load_x = pltpu.make_async_copy(x_hbm, x_ref, lsem.at[0])
    load_x.start()
    loads = []
    for k, head in enumerate(targets):
        group = []
        for i, w in enumerate((wq_hbm, wk_hbm, wv_hbm)):
            at = (3 * k + i) * HD
            load = pltpu.make_async_copy(
                w.at[:, tile_at(head, HD)], wf_ref.at[:, at : at + HD], wsem.at[k, i]
            )
            load.start()
            group.append(load)
        loads.append(group)
    load_wo = pltpu.make_async_copy(wo_hbm, wo_ref, lsem.at[1])
    load_wo.start()
    load_wi = pltpu.make_async_copy(wi_hbm, wi_ref, lsem.at[2])
    load_wi.start()
    load_teacher = pltpu.make_async_copy(teacher_hbm, mix_ref, lsem.at[3])
    load_teacher.start()
    load_wf = pltpu.make_async_copy(wf_hbm, wf_ref, lsem.at[4])
    others = [(d, target, t) for target in targets[:3]] + [(1 - d, target, t) for target in targets]
    greet(others, True)
    all_ids_ref[d, c] = ids_ref[...]
    id_copies = []
    for i, other in enumerate(others):
        copy = remote(ids_ref, all_ids_ref.at[d, c], isem.at[i], jsem.at[i], other)
        copy.start()
        id_copies.append(copy)
    sums_ref[...] = jnp.zeros_like(sums_ref)
    bsum_ref[...] = jnp.zeros_like(bsum_ref)
    error_ref[...] = jnp.zeros_like(error_ref)
    load_x.wait()

    here = tile_at(c, span)

    def project_copy(k, s):
        return remote(
            psend.at[k, s], qkv_ref.at[:, s, here, :], pssem.at[k, s], prsem.at[k, s], peers[k]
        )

    for s in range(2):
        for k, head in enumerate(targets):
            if s == 0:
                for load in loads[k]:
                    load.wait()
            value = dot(
                x_ref[s * span : (s + 1) * span, :], wf_ref[:, 3 * k * HD : 3 * (k + 1) * HD]
            )
            for i in range(3):
                part = (value[:, i * HD : (i + 1) * HD] + bias_ref[i, head]).astype(BF16)
                if k < 3:
                    psend[k, s, i] = part
                else:
                    qkv_ref[i, s, here, :] = part
            if k < 3:
                project_copy(k, s).start()
    load_wf.start()
    for copy in id_copies:
        copy.wait()

    mine = tile_at(c, HD)
    scale = HD ** (-0.5)

    def attended_copy(k, s):
        return remote(
            osend.at[k, s],
            o_ref.at[pl.ds(s * span, span), mine],
            ossem.at[k, s],
            orsem.at[k, s],
            peers[k],
        )

    def receive(s):
        def run():
            for k in range(3):
                project_copy(k, s).wait_recv()

        return run

    def attend_block(s, k):
        def run():
            rows = tile_at(targets[k], span)
            key_row = jnp.concatenate(
                [all_ids_ref[d, cc, s : s + 1, :] for cc in range(4)], axis=1
            ).astype(F32)
            own = id_columns(all_ids_ref[d, targets[k], s : s + 1, :].astype(F32))
            score = dot_nt(qkv_ref[0, s, rows, :], qkv_ref[1, s]) * scale
            score = jnp.where(own == key_row, score, -1e30)
            top = jnp.max(score, axis=-1, keepdims=True)
            lse = top + jnp.log(jnp.sum(jnp.exp(score - top), axis=-1, keepdims=True))
            lse_ref[s, rows, :] = lse
            weights = jnp.exp(score - lse).astype(BF16)
            block = dot(weights, qkv_ref[2, s]).astype(BF16)
            if k < 3:
                osend[k, s] = block
                attended_copy(k, s).start()
            else:
                o_ref[s * span : (s + 1) * span, mine] = block

        return run

    def attended(s):
        def run():
            for k in range(3):
                attended_copy(k, s).wait_recv()

        return run

    columns = width // (2 * PIECES)

    def columns_at(half, piece):
        return tile_at(half * PIECES + piece, columns)

    def of_attention(s):
        return lambda half, piece: dot(
            o_ref[s * span : (s + 1) * span, :], wo_ref[:, columns_at(half, piece)]
        )

    def of_hidden(s):
        return lambda half, piece: dot(
            act_ref[s * span : (s + 1) * span, :], wf_ref[:, columns_at(half, piece)]
        )

    def of_back(s):
        return lambda half, piece: dot_nt(
            slope_ref[s * span : (s + 1) * span, :], wi_ref[columns_at(half, piece), :]
        )

    count = len(refs) - SCATTER_REFS
    sets = (refs[: count // 2], refs[count // 2 : count])
    produces = [make(s) for make in (of_attention, of_hidden, of_back) for s in range(2)]
    lines = [Line(sets[k % 2], produce) for k, produce in enumerate(produces)]

    def first_norm(s):
        line = lines[s]

        def run():
            line.arrived()

            def body(start):
                rows = pl.ds(s * span + start, STEP_ROWS)
                first = x_ref[rows, :].astype(F32) + (line.rows(start) + vec_ref[0:1, :])
                center = first - mean_last(first)
                rstd = lax.rsqrt(mean_last(center * center) + 1e-05)
                value = center * rstd
                norm_ref[rows, :] = value.astype(BF16)
                rstd_ref[rows, :] = rstd
                low_ref[rows, :] = (value * vec_ref[1:2, :] + vec_ref[2:3, :]).astype(BF16)

            each_block(span, body)

        return run

    block = 256

    def up(s, first, last):
        rows = slice(s * span, (s + 1) * span)

        def run():
            def body(j, carry):
                cols = tile_at(j, block)
                u = dot(low_ref[rows, :], wi_ref[:, cols]) + bi_ref[0:1, cols]
                square = u * u
                th = jnp.tanh(GELU_A * (u + 0.044715 * (u * square)))
                act_ref[rows, cols] = (0.5 * u * (1.0 + th)).astype(BF16)
                slope_ref[rows, cols] = (
                    0.5 * (1.0 + th)
                    + 0.5 * u * (1.0 - th * th) * (GELU_A * (1.0 + 3.0 * 0.044715 * square))
                ).astype(BF16)
                return carry

            lax.fori_loop(first, last, body, 0)

        return run

    def second_norm(s):
        line = lines[2 + s]

        def run():
            line.arrived()
            total_count = jnp.sum((all_ids_ref[...] > 0).astype(F32))
            factor = 2.0 * (2 * 4 * 2 * span) / total_count

            def body(start):
                rows = pl.ds(s * span + start, STEP_ROWS)
                second = norm_ref[rows, :].astype(F32) * vec_ref[1:2, :] + vec_ref[2:3, :]
                second = second + (line.rows(start) + vec_ref[3:4, :])
                center = second - mean_last(second)
                rstd = lax.rsqrt(mean_last(center * center) + 1e-05)
                value = center * rstd
                result = value * vec_ref[4:5, :] + vec_ref[5:6, :]
                x_ref[rows, :] = result.astype(BF16)
                gap = (result - mix_ref[rows, :].astype(F32)) * valid_ref[rows, :]
                error_ref[...] += fold(gap * gap)
                d_result = gap * factor
                sums_ref[0] += fold(d_result * value)
                sums_ref[1] += fold(d_result)
                d_value = d_result * vec_ref[4:5, :]
                d_second = (d_value - mean_last(d_value) - value * mean_last(d_value * value)) * rstd
                d_low = d_second.astype(BF16)
                dlow_ref[rows, :] = d_low
                sums_ref[2] += fold(d_low.astype(F32))

            each_block(span, body)

        return run

    def down(s, first, last):
        rows = slice(s * span, (s + 1) * span)

        def run():
            def body(j, carry):
                cols = tile_at(j, block)
                d_act = dot_nt(dlow_ref[rows, :], wf_ref[cols, :])
                d_pre = (d_act * slope_ref[rows, cols].astype(F32)).astype(BF16)
                slope_ref[rows, cols] = d_pre
                bsum_ref[:, cols] += fold(d_pre.astype(F32))
                return carry

            lax.fori_loop(first, last, body, 0)

        return run

    def first_back(s):
        line = lines[4 + s]

        def run():
            line.arrived()

            def body(start):
                rows = pl.ds(s * span + start, STEP_ROWS)
                value = norm_ref[rows, :].astype(F32)
                d_normed = dlow_ref[rows, :].astype(F32) + line.rows(start)
                sums_ref[3] += fold(d_normed * value)
                sums_ref[4] += fold(d_normed)
                d_value = d_normed * vec_ref[1:2, :]
                d_first = d_value - mean_last(d_value) - value * mean_last(d_value * value)
                d_low = (d_first * rstd_ref[rows, :]).astype(BF16)
                mix_ref[rows, :] = d_low
                sums_ref[5] += fold(d_low.astype(F32))

            each_block(span, body)

        return run

    narrow = gouter_ref.shape[1]
    tall = refs[count].shape[2]

    def outer_tile(core, ctx, tile):
        return dot_tn(act_ref[:, tile_at(tile, tall)], dlow_ref[:, tile_at(core * 4 + ctx, narrow)])

    def outer_write(tile, value):
        gouter_ref[tile_at(tile, tall), :] = value

    outer = Scatter(
        outer_tile, lambda tile: gouter_ref[tile_at(tile, tall), :], outer_write, refs[count:]
    )
    pairs = outer.pairs()
    receive(0)()
    for k in range(4):
        attend_block(0, k)()
    attended(0)()
    load_wo.wait()
    pieces = local // block
    a, b, e = 2 * pieces // 8, 5 * pieces // 8, pieces
    tasks = [
        [(0, receive(1))] + [(k, attend_block(1, k)) for k in range(4)] + [(7, attended(1))],
        [(4, first_norm(0)), (5, load_wi.wait), (5, up(0, 0, a)), (6, up(0, a, b)), (7, up(0, b, e)), (7, lines[0].drain), (7, load_wf.wait)],
        [(4, first_norm(1)), (5, up(1, 0, a)), (6, up(1, a, b)), (7, up(1, b, e)), (7, lines[1].drain), (3, load_teacher.wait)],
        [(4, second_norm(0)), (5, down(0, 0, a)), (6, down(0, a, b)), (7, down(0, b, e)), (7, lines[2].drain)],
        [(4, second_norm(1)), (5, down(1, 0, a)), (5, lambda: outer.give(0)), (6, down(1, a, b)), (6, pairs[0]), (7, down(1, b, e)), (7, lines[3].drain)],
        [(0, pairs[1]), (1, pairs[2]), (2, pairs[3]), (4, first_back(0)), (7, lines[4].drain)],
    ]
    run_stream(lines, tasks)
    stores = [
        pltpu.make_async_copy(qkv_ref, qkv_hbm, lsem.at[0]),
        pltpu.make_async_copy(o_ref, o_hbm, lsem.at[1]),
        pltpu.make_async_copy(low_ref, low_hbm, lsem.at[2]),
        pltpu.make_async_copy(x_ref, out_hbm, lsem.at[3]),
        pltpu.make_async_copy(slope_ref, dpre_hbm, lsem.at[4]),
    ]
    for store in stores:
        store.start()
    first_back(1)()
    store_mix = pltpu.make_async_copy(mix_ref, dmix_hbm, lsem.at[5])
    store_mix.start()
    lines[5].drain()
    outer.finish()
    store_outer = pltpu.make_async_copy(gouter_ref, gouter_hbm, lsem.at[6])
    store_outer.start()
    for k in range(3):
        for s in range(2):
            project_copy(k, s).wait_send()
            attended_copy(k, s).wait_send()
    for store in stores + [store_mix, store_outer]:
        store.wait()


def forward(inputs, ids, valid, w_query, w_key, w_value, bias, w_output, w_inner, b_inner, w_outer, teacher, vectors):
    seqs, span = ids.shape
    rows, width = inputs.shape
    local = w_inner.shape[1]
    heads = w_output.shape[0]
    length = 4 * span
    vmem = pl.BlockSpec(memory_space=pltpu.VMEM)
    hbm = pl.BlockSpec(memory_space=pl.ANY)
    shape = jax.ShapeDtypeStruct
    semaphores = pltpu.SemaphoreType.DMA
    return pl.pallas_call(
        forward_kernel,
        out_shape=(
            shape((2, 4, seqs, span), jnp.int32),
            shape((3, seqs, length, HD), BF16),
            shape((seqs, length, 1), F32),
            shape((rows, heads), BF16),
            shape((rows, width), BF16),
            shape((rows, width), BF16),
            shape((rows, local), BF16),
            shape((rows, width), BF16),
            shape((6, 8, width), F32),
            shape((8, local), F32),
            shape((8, width), F32),
            shape((local, width // 8), F32),
        ),
        in_specs=[hbm, vmem, vmem, hbm, hbm, hbm, vmem, hbm, hbm, vmem, hbm, hbm, vmem],
        out_specs=(vmem, hbm, vmem, hbm, hbm, hbm, hbm, hbm, vmem, vmem, vmem, hbm),
        scratch_shapes=[
            pltpu.VMEM((rows, width), BF16),
            pltpu.VMEM((local, width), BF16),
            pltpu.VMEM((width, local), BF16),
            pltpu.VMEM((heads, width), BF16),
            pltpu.VMEM((3, seqs, length, HD), BF16),
            pltpu.VMEM((3, seqs, 3, span, HD), BF16),
            pltpu.VMEM((rows, heads), BF16),
            pltpu.VMEM((3, seqs, span, HD), BF16),
            pltpu.VMEM((rows, width), BF16),
            pltpu.VMEM((rows, 1), F32),
            pltpu.VMEM((rows, width), BF16),
            pltpu.VMEM((rows, local), BF16),
            pltpu.VMEM((rows, local), BF16),
            pltpu.VMEM((rows, width), BF16),
            pltpu.VMEM((rows, width), BF16),
            pltpu.VMEM((local, width // 8), F32),
            semaphores((7,)),
            semaphores((4, 3)),
            semaphores((3, seqs)),
            semaphores((3, seqs)),
            semaphores((7,)),
            semaphores((7,)),
            semaphores((3, seqs)),
            semaphores((3, seqs)),
        ]
        + stream_scratch(span, width)
        + stream_scratch(span, width)
        + scatter_scratch(4, local // 4, width // 8),
        compiler_params=pltpu.CompilerParams(
            collective_id=0, has_side_effects=True, vmem_limit_bytes=VMEM_BYTES
        ),
        name="forward",
    )(inputs, ids, valid, w_query, w_key, w_value, bias, w_output, w_inner, b_inner, w_outer, teacher, vectors)


def attend_back_kernel(
    dmix_ref, wo_ref, qkv_ref, lse_ref, ids_ref, wq_hbm, wk_hbm, wv_hbm, sums_ref, bsum_ref, error_ref, o_ref, x_ref, low_ref, dpre_hbm,
    grad_hbm, small_ref, loss_ref, goutput_ref, gqkv_ref, ginner_ref,
    drows_ref, dpre_ref, d_all, dsend, dkv, gsend, w_refs, stage, pack, packs, lsem, gsem, ssem, rsem, gssem, grsem, pssem, prsem,
    *refs,
):
    d, c, t = place()
    line, refs = refs[:LINE_REFS], refs[LINE_REFS:]
    loads = [
        pltpu.make_async_copy(ref, w_refs.at[i], lsem.at[i])
        for i, ref in enumerate((wq_hbm, wk_hbm, wv_hbm))
    ] + [
        pltpu.make_async_copy(dpre_hbm, dpre_ref, lsem.at[3]),
    ]
    for load in loads:
        load.start()
    span = dmix_ref.shape[0] // 2
    peers = ctx_peers()
    others = peers + [(1 - d, cc, t) for cc in (peers[0][1], peers[1][1], peers[2][1], c)]
    greet(others, True)
    targets = [peer[1] for peer in peers] + [c]
    mine = pl.ds(pl.multiple_of(c * HD, HD), HD)
    here = pl.ds(pl.multiple_of(c * span, span), span)
    copies = []
    for k, target in enumerate(targets):
        wide = wo_ref[pl.ds(pl.multiple_of(target * HD, HD), HD), :]
        for s in range(2):
            block = dot_nt(dmix_ref[s * span : (s + 1) * span, :], wide).astype(BF16)
            if k < 3:
                dsend[k, s] = block
            else:
                d_all[s, here, :] = block
        if k < 3:
            copy = remote(dsend.at[k], d_all.at[:, here, :], ssem.at[k], rsem.at[k], peers[k])
            copy.start()
            copies.append(copy)
    narrow = goutput_ref.shape[1]

    def output_write(tile, value):
        goutput_ref[...] = value

    output = Scatter(
        lambda core, ctx, tile: dot_tn(o_ref[...], dmix_ref[:, tile_at(core * 4 + ctx, narrow)]),
        lambda tile: goutput_ref[...],
        output_write,
        refs[:SCATTER_REFS],
    )
    output.give(0)
    for task in output.pairs():
        task()
    for copy in copies:
        copy.wait()
    scale = HD ** (-0.5)
    copies = []
    for s in range(2):
        rows_here = pl.ds(s * span, span)
        key_row = jnp.concatenate([ids_ref[d, cc, s : s + 1, :] for cc in range(4)], axis=1)
        keys = qkv_ref[1, s]
        values = qkv_ref[2, s]
        for k, target in enumerate(targets):
            rows = pl.ds(pl.multiple_of(target * span, span), span)
            own = id_columns(ids_ref[d, target, s : s + 1, :].astype(F32))
            queries = qkv_ref[0, s, rows, :]
            score = dot_nt(queries, keys) * scale
            score = jnp.where(own == key_row.astype(F32), score, -1e30)
            probs = jnp.exp(score - lse_ref[s, rows, :])
            d_out = d_all[s, rows, :]
            d_probs = dot_nt(d_out, values)
            inner = jnp.sum(probs * d_probs, axis=-1, keepdims=True)
            d_score = (probs * (d_probs - inner)).astype(BF16)
            d_query = (dot(d_score, keys) * scale).astype(BF16)
            d_key = dot_tn(d_score, queries)
            d_value = dot_tn(probs.astype(BF16), d_out)
            if k == 0:
                dkv[0] = d_key
                dkv[1] = d_value
            else:
                dkv[0] += d_key
                dkv[1] += d_value
            if k < 3:
                gsend[0, k, s] = d_query
                copy = remote(
                    gsend.at[0, k, s],
                    drows_ref.at[0, rows_here, mine],
                    gssem.at[0, k, s],
                    grsem.at[0, k, s],
                    peers[k],
                )
                copy.start()
                copies.append(copy)
            else:
                drows_ref[0, rows_here, mine] = d_query
        for k, target in enumerate(targets):
            rows = pl.ds(pl.multiple_of(target * span, span), span)
            for i, factor in ((0, scale), (1, 1.0)):
                block = (dkv[i, rows, :] * factor).astype(BF16)
                if k < 3:
                    gsend[1 + i, k, s] = block
                    copy = remote(
                        gsend.at[1 + i, k, s],
                        drows_ref.at[1 + i, rows_here, mine],
                        gssem.at[1 + i, k, s],
                        grsem.at[1 + i, k, s],
                        peers[k],
                    )
                    copy.start()
                    copies.append(copy)
                else:
                    drows_ref[1 + i, rows_here, mine] = block
    for copy in copies:
        copy.wait()
    for i in range(6):
        pack[i : i + 1, :] = jnp.sum(sums_ref[i], axis=0, keepdims=True)
    pack[6:7, :] = jnp.sum(bsum_ref[...], axis=0, keepdims=True)
    lanes = drows_ref.shape[2]
    pack[7:8, 0:lanes] = jnp.sum(drows_ref[0].astype(F32), axis=0, keepdims=True)
    pack[7:8, lanes : 2 * lanes] = jnp.sum(drows_ref[2].astype(F32), axis=0, keepdims=True)
    error = jnp.sum(error_ref[...])
    pack[7:8, 2 * lanes : 4 * lanes] = jnp.full((1, 2 * lanes), error, F32)
    small_copies = []
    for i, other in enumerate(others):
        copy = remote(pack, packs.at[d, c], pssem.at[i], prsem.at[i], other)
        copy.start()
        small_copies.append(copy)
    for load in loads:
        load.wait()
    columns = line[3].shape[3]

    def produce(half, chunk):
        cols = pl.ds(pl.multiple_of(chunk * columns, columns), columns)
        rows = tile_at(half, span)
        return (
            dot_nt(drows_ref[0, rows, :], w_refs[0, cols, :])
            + dot_nt(drows_ref[1, rows, :], w_refs[1, cols, :])
            + dot_nt(drows_ref[2, rows, :], w_refs[2, cols, :])
        )

    deep = gqkv_ref.shape[1]

    def qkv_write(tile, value):
        gqkv_ref[tile] = value

    qkv_grad = Scatter(
        lambda core, ctx, tile: dot_tn(x_ref[:, tile_at(core * 4 + ctx, deep)], drows_ref[tile]),
        lambda tile: gqkv_ref[tile],
        qkv_write,
        refs[SCATTER_REFS : 2 * SCATTER_REFS],
    )
    wide = refs[2 * SCATTER_REFS].shape[3]

    def inner_tile(core, ctx, tile):
        return dot_tn(low_ref[:, tile_at(core * 4 + ctx, deep)], dpre_ref[:, tile_at(tile, wide)])

    def inner_write(tile, value):
        ginner_ref[:, tile_at(tile, wide)] = value

    inner = Scatter(
        inner_tile,
        lambda tile: ginner_ref[:, tile_at(tile, wide)],
        inner_write,
        refs[2 * SCATTER_REFS :],
    )
    qkv_grad.give(0)
    tasks = list(enumerate(qkv_grad.pairs())) + [(3, lambda: inner.give(0))]
    tasks += [(4 + i, task) for i, task in enumerate(inner.pairs())]
    line_sum(produce, line, tasks)

    def finish(step, carry):
        rows = rows_at(step)
        slot = lax.rem(step, 2)

        def store(at):
            return pltpu.make_async_copy(stage.at[slot], grad_hbm.at[rows_at(at), :], gsem.at[slot])

        @pl.when(step >= 2)
        def _():
            store(step - 2).wait()

        stage[slot] = dmix_ref[rows, :].astype(F32) + row_block(line[3], step)
        store(step).start()
        return carry

    steps = dmix_ref.shape[0] // STEP_ROWS
    lax.fori_loop(0, steps, finish, 0)
    for i in range(2):
        pltpu.make_async_copy(
            stage.at[i], grad_hbm.at[pl.ds((steps - 2 + i) * STEP_ROWS, STEP_ROWS), :], gsem.at[i]
        ).wait()
    output.finish()
    qkv_grad.finish()
    inner.finish()
    for copy in small_copies:
        copy.wait()
    packs[d, c] = pack[...]
    small = jnp.zeros_like(pack)
    for i in range(2):
        for j in range(4):
            small = small + packs[i, j]
    small_ref[...] = small
    count = jnp.sum((ids_ref[...] > 0).astype(F32))
    loss_ref[...] = jnp.broadcast_to(small[7:8, 2 * lanes : 2 * lanes + 128] / count, (8, 128))


def attend_back(
    d_mix, w_output, qkv, lse, all_ids, w_query, w_key, w_value, sums, inner_sum, error, attn_rows, inputs, low, d_pre
):
    rows, width = d_mix.shape
    local = w_query.shape[1]
    seqs, length = qkv.shape[1], qkv.shape[2]
    span = rows // seqs
    vmem = pl.BlockSpec(memory_space=pltpu.VMEM)
    hbm = pl.BlockSpec(memory_space=pl.ANY)
    return pl.pallas_call(
        attend_back_kernel,
        out_shape=(
            jax.ShapeDtypeStruct((rows, width), F32),
            jax.ShapeDtypeStruct((8, width), F32),
            jax.ShapeDtypeStruct((8, 128), F32),
            jax.ShapeDtypeStruct((local, width // 8), F32),
            jax.ShapeDtypeStruct((3, width // 8, local), F32),
            jax.ShapeDtypeStruct((width // 8, d_pre.shape[1]), F32),
        ),
        in_specs=[vmem] * 5 + [hbm] * 3 + [vmem] * 6 + [hbm],
        out_specs=(hbm,) + (vmem,) * 5,
        scratch_shapes=[
            pltpu.VMEM((3, rows, local), BF16),
            pltpu.VMEM((rows, d_pre.shape[1]), BF16),
            pltpu.VMEM((seqs, length, HD), BF16),
            pltpu.VMEM((3, seqs, span, HD), BF16),
            pltpu.VMEM((2, length, HD), F32),
            pltpu.VMEM((3, 3, seqs, span, HD), BF16),
            pltpu.VMEM((3, width, local), BF16),
            pltpu.VMEM((2, STEP_ROWS, width), F32),
            pltpu.VMEM((8, width), F32),
            pltpu.VMEM((2, 4, 8, width), F32),
            pltpu.SemaphoreType.DMA((4,)),
            pltpu.SemaphoreType.DMA((2,)),
            pltpu.SemaphoreType.DMA((3,)),
            pltpu.SemaphoreType.DMA((3,)),
            pltpu.SemaphoreType.DMA((3, 3, seqs)),
            pltpu.SemaphoreType.DMA((3, 3, seqs)),
            pltpu.SemaphoreType.DMA((7,)),
            pltpu.SemaphoreType.DMA((7,)),
        ]
        + line_scratch(rows, width)
        + scatter_scratch(1, local, width // 8)
        + scatter_scratch(3, width // 8, local)
        + scatter_scratch(4, width // 8, d_pre.shape[1] // 4),
        compiler_params=pltpu.CompilerParams(
            collective_id=4, has_side_effects=True, vmem_limit_bytes=VMEM_BYTES
        ),
        name="attend_back",
    )(
        d_mix, w_output, qkv, lse, all_ids, w_query, w_key, w_value, sums, inner_sum, error, attn_rows, inputs, low, d_pre
    )


def quick_shards(
    hidden_in,
    segment_ids,
    teacher,
    w_query,
    b_query,
    w_key,
    w_value,
    b_value,
    w_output,
    b_output,
    first_gain,
    first_shift,
    w_inner,
    b_inner,
    w_outer,
    b_outer,
    second_gain,
    second_shift,
):
    seq_count, span_len, width = hidden_in.shape
    rows = seq_count * span_len
    local = w_query.shape[1]
    inputs = hidden_in.reshape(rows, width)
    bias = jnp.stack([b_query, jnp.zeros_like(b_query), b_value]).reshape(3, local // HD, 1, HD)
    valid = (segment_ids.reshape(rows, 1) > 0).astype(F32)
    vectors = jnp.stack([b_output, first_gain, first_shift, b_outer, second_gain, second_shift])
    (
        all_ids,
        qkv,
        lse,
        attn_rows,
        normed_low,
        layer_out,
        d_pre,
        d_mix,
        sums,
        inner_sum,
        error,
        grad_w_outer,
    ) = forward(
        inputs,
        segment_ids,
        valid,
        w_query,
        w_key,
        w_value,
        bias,
        w_output,
        w_inner,
        b_inner.reshape(1, -1),
        w_outer,
        teacher.reshape(rows, width),
        vectors,
    )
    grad_input, small, loss, grad_w_output, grad_qkv, grad_w_inner = attend_back(
        d_mix,
        w_output,
        qkv,
        lse,
        all_ids,
        w_query,
        w_key,
        w_value,
        sums,
        inner_sum,
        error,
        attn_rows,
        inputs,
        normed_low,
        d_pre,
    )
    grad_w_query, grad_w_key, grad_w_value = grad_qkv[0], grad_qkv[1], grad_qkv[2]
    shape = (seq_count, span_len, width)
    return (
        layer_out.reshape(shape),
        loss[0, 0],
        grad_input.reshape(shape),
        grad_w_query,
        small[7, :local],
        grad_w_key,
        grad_w_value,
        small[7, local : 2 * local],
        grad_w_output,
        small[5],
        small[3],
        small[4],
        grad_w_inner,
        small[6],
        grad_w_outer,
        small[2],
        small[0],
        small[1],
    )


def chosen(*args):
    seq_count, span_len, width = args[0].shape
    local_heads = args[3].shape[1] // HD
    fits = (
        seq_count == 2
        and lax.axis_size("dp") == 2
        and lax.axis_size("ctx") == 4
        and local_heads == 4
        and args[12].shape[1] == width
        and 4 * args[3].shape[1] == width
    )
    return quick_shards(*args) if fits else shards(*args)


def solution(mesh):
    placed = (
        P("dp", "ctx", None),
        P("dp", "ctx"),
        P("dp", "ctx", None),
        P(None, "tensor"),
        P("tensor"),
        P(None, "tensor"),
        P(None, "tensor"),
        P("tensor"),
        P("tensor", None),
        P(),
        P(),
        P(),
        P(None, "tensor"),
        P("tensor"),
        P("tensor", None),
        P(),
        P(),
        P(),
    )
    return jax.shard_map(
        chosen,
        mesh=mesh,
        in_specs=placed,
        out_specs=(
            P("dp", "ctx", None),
            P(),
            P("dp", "ctx", None),
            P(("dp", "ctx"), "tensor"),
            P("tensor"),
            P(("dp", "ctx"), "tensor"),
            P(("dp", "ctx"), "tensor"),
            P("tensor"),
            P("tensor", ("dp", "ctx")),
            P(),
            P(),
            P(),
            P(("dp", "ctx"), "tensor"),
            P("tensor"),
            P("tensor", ("dp", "ctx")),
            P(),
            P(),
            P(),
        ),
        check_vma=False,
    )
```
